32 devices in a mesh: ev: 32 (over z, y, x, core).
Axes of the slice: x: 2, y: 2, z: 4, core: 2. Of those that a mesh axis runs over, the one named last changes fastest.
Arguments:
- records: bfloat16 [4096, 512], P('ev'), may hold values from -16 to 16
- filter_taps: bfloat16 [65], replicated, may hold values from -0.75 to 0.75
- live_counts: int32 [32], P('ev'), may hold values from 64 to 128, as said below
- pair_valid: int32 [32, 9], P('ev'), may hold values 0 or 1
Outputs:
- correlations: bfloat16 [4096, 10, 25, 128], P('ev')
The draws below stay inside these ranges and needn't reach their ends.
Inputs may be any that keep to these rules, and one draw needn't show every extreme that they name: The first live_counts[b] events of block b are live and its other rows are padding; some block has all 128 events live.
All inputs are finite; a program needn't handle non-finite values. No bound on the sum of `pair_valid` on one device may be relied on, other than what follows from the above.
Results may differ from the reference program's by a relative error of at most 0.0047.
Values may be sent and summed in bfloat16 or wider, within the bound.
A program may use at most 64 MiB of HBM per device.

```python
import math
import jax
import jax.numpy as jnp
from jax import lax

EB = 128
W = 512
TAPS = 65
HALF = 12
REACH = 9
BLOCKS = 32
EVENTS = 4096


def draw_records(key, part):
    scale_key = jax.random.fold_in(key, 11)
    shape_key = jax.random.fold_in(key, 12)
    amplitude = jnp.exp(jax.random.uniform(scale_key, (EVENTS, 1), jnp.float32, math.log(0.3), math.log(3.0)))
    values = amplitude * jax.random.normal(shape_key, (EVENTS, W), jnp.float32)
    return jnp.clip(values, -16.0, 16.0).astype(jnp.bfloat16)


def draw_live_counts(key, part):
    count_key = jax.random.fold_in(key, 21)
    full_key = jax.random.fold_in(key, 22)
    counts = jax.random.randint(count_key, (BLOCKS,), EB // 2, EB + 1)
    full_block = jax.random.randint(full_key, (), 0, BLOCKS)
    positions = jnp.arange(BLOCKS, dtype=jnp.int32)
    return jnp.where(positions == full_block, EB, counts).astype(jnp.int32)


def place_ends(drawn, own_key, smallest, high):
    place = [jax.random.randint(jax.random.fold_in(own_key, axis), (), 0, length) for axis, length in enumerate(drawn.shape)]
    widest = drawn.shape.index(max(drawn.shape))
    neighbour = place[:widest] + [(place[widest] + 1) % drawn.shape[widest]] + place[widest + 1:]
    return drawn.at[tuple(place)].set(smallest).at[tuple(neighbour)].set(high)


def gaussian(stream_key, shape, deviation, bound, held_as=jnp.bfloat16):
    return jnp.clip(deviation * jax.random.normal(stream_key, shape, jnp.float32), -bound, bound).astype(held_as)


def setup_inputs(seed: int = 0) -> dict:
    key_of = jax.random.split(jax.random.key(seed), 5)
    return {
        "records": draw_records(jax.random.fold_in(key_of[4], 71), 0),
        "filter_taps": gaussian(key_of[1], (TAPS,), TAPS ** -0.5, 0.75),
        "live_counts": draw_live_counts(jax.random.fold_in(key_of[4], 71), 0),
        "pair_valid": place_ends((jax.random.randint(key_of[3], (BLOCKS, REACH), 0, 4) < 3).astype(jnp.int32), jax.random.fold_in(key_of[3], 1), 0, 1),
    }


epsilon = 1e-06

def band_matrix(filter_taps, samples):
    half_taps = (filter_taps.shape[0] - 1) // 2
    period = 2 * samples - 1
    spread = jnp.zeros((period,), jnp.float32)
    spread = lax.dynamic_update_slice(spread, filter_taps.astype(jnp.float32), (samples - 1 - half_taps,))
    repeated = jnp.tile(spread, samples + 1)[:samples * (period + 1)]
    hankel = repeated.reshape(samples, period + 1)[:, :samples]
    return hankel[:, ::-1].astype(jnp.bfloat16)

def correlate(own_block, own_scale, partner, weight):
    samples = own_block.shape[1]
    partner_scale = lax.rsqrt(lax.optimization_barrier(jnp.sum(jnp.square(partner.astype(jnp.float32)), axis=1)) + epsilon)
    padded = jnp.pad(partner, ((0, 0), (HALF, HALF)))
    products = [lax.dot_general(own_block, padded[:, lag_index:lag_index + samples], (((1,), (1,)), ((), ())), preferred_element_type=jnp.float32) for lag_index in range(2 * HALF + 1)]
    stacked = jnp.stack(products, axis=1)
    return (stacked * own_scale[:, None, None] * partner_scale[None, None, :] * weight).astype(jnp.bfloat16)

def reference(records, filter_taps, live_counts, pair_valid):
    blocked = records.reshape(BLOCKS, EB, W)
    live_rows = jnp.arange(EB, dtype=jnp.int32)[None, :] < live_counts[:, None]
    kept_rows = jnp.where(live_rows[:, :, None], blocked, jnp.zeros((), records.dtype))
    matrix = band_matrix(filter_taps, W)
    filtered = jnp.dot(kept_rows.reshape(EVENTS, W), matrix, preferred_element_type=jnp.float32).astype(jnp.bfloat16).reshape(BLOCKS, EB, W)
    scales = lax.rsqrt(lax.optimization_barrier(jnp.sum(jnp.square(filtered.astype(jnp.float32)), axis=2)) + epsilon)
    extended = jnp.concatenate([filtered, jnp.zeros((REACH, EB, W), filtered.dtype)], axis=0)

    def one_block(block_index):
        own_block = filtered[block_index]
        own_scale = scales[block_index]
        pieces = []
        for distance in range(REACH + 1):
            partner = lax.dynamic_index_in_dim(extended, block_index + distance, 0, keepdims=False)
            if distance == 0:
                weight = jnp.ones((), jnp.float32)
            else:
                weight = pair_valid[block_index, distance - 1].astype(jnp.float32)
            pieces.append(correlate(own_block, own_scale, partner, weight))
        return jnp.stack(pieces, axis=1)
    result = lax.map(one_block, jnp.arange(BLOCKS, dtype=jnp.int32))
    return result.reshape(EVENTS, REACH + 1, 2 * HALF + 1, EB)
```

```python
import functools

import jax
import jax.numpy as jnp
from jax import lax
from jax.experimental import pallas as pl
from jax.experimental.pallas import tpu as pltpu
from jax.sharding import PartitionSpec as P

HALF = 12
LAGS = 2 * HALF + 1
LAGS_AT_ONCE = 5
LANES = 128

epsilon = 1e-06

NT = (((1,), (1,)), ((), ()))
NN = (((1,), (0,)), ((), ()))


def split_squares(block):
    wide = block.astype(jnp.float32)
    square = wide * wide
    high = square.astype(jnp.bfloat16)
    low = (square - high.astype(jnp.float32)).astype(jnp.bfloat16)
    return high, low


def kernel(
    devices, records, taps, live_count, pair_valid, out,
    held, shifted, spread, row_scale, scale,
    z_sem, layer_sem, ten_sem, pair_sem, recv_sem,
):
    events, samples = records.shape
    reach = pair_valid.shape[1]
    half_taps = (taps.shape[1] - 1) // 2
    per_layer = (reach - 1) // 2
    far = reach - 1
    last = reach + 1
    chips = devices // 2
    me = lax.axis_index("ev")
    core = lax.rem(me, 2)
    chip = me // 2
    place = lax.rem(chip, per_layer)
    sibling = me + 1 - 2 * core

    def in_layer(d):
        return me - 2 * place + 2 * lax.rem(place + per_layer - d, per_layer)

    barrier = pltpu.get_barrier_semaphore()

    def greet(device):
        pl.semaphore_signal(
            barrier, inc=1, device_id=(device,), device_id_type=pl.DeviceIdType.MESH
        )

    has_down = chip >= per_layer
    has_up = chip + per_layer < chips
    down_edge = (core == 0) & (place == 0) & (chip >= 1)
    up_edge = (core == 0) & (place == per_layer - 1) & (chip + 1 < chips)
    greet(sibling)
    for d in range(1, per_layer):
        greet(in_layer(d))

    @pl.when(has_down)
    def _():
        greet(me - 2 * per_layer)

    @pl.when(has_up)
    def _():
        greet(me + 2 * per_layer)

    @pl.when(down_edge)
    def _():
        greet(me - 2)

    @pl.when(up_edge)
    def _():
        greet(me + 2)

    spread[...] = jnp.zeros_like(spread)
    spread[0:1, 0 : taps.shape[1]] = taps[...].astype(jnp.float32)
    rolled = pltpu.roll(
        jnp.broadcast_to(spread[0:1, :], (samples, samples)),
        samples - half_taps, 1, stride=1, stride_axis=0,
    )
    t = lax.broadcasted_iota(jnp.int32, (samples, samples), 0)
    u = lax.broadcasted_iota(jnp.int32, (samples, samples), 1)
    band = jnp.where(jnp.abs(u - t) <= half_taps, rolled, 0.0).astype(jnp.bfloat16)
    row = lax.broadcasted_iota(jnp.int32, (events, samples), 0)
    kept = jnp.where(row < live_count[0], records[...].astype(jnp.float32), 0.0)
    own = lax.dot_general(
        kept.astype(jnp.bfloat16), band, NT, preferred_element_type=jnp.float32
    ).astype(jnp.bfloat16)
    held[0] = own

    for k in range(1, last + 1):
        if k == last:
            missing = (core == 0) & (me + k >= devices)
        else:
            missing = me + k >= devices

        @pl.when(missing)
        def _(k=k):
            held[k] = jnp.zeros((events, samples), jnp.bfloat16)

    greeted = (
        per_layer
        + has_down.astype(jnp.int32)
        + has_up.astype(jnp.int32)
        + down_edge.astype(jnp.int32)
        + up_edge.astype(jnp.int32)
    )
    pl.semaphore_wait(barrier, greeted)

    def remote(source, slot, send_sem, device):
        return pltpu.make_async_remote_copy(
            src_ref=held.at[source],
            dst_ref=held.at[slot],
            send_sem=send_sem,
            recv_sem=recv_sem.at[slot],
            device_id=(device,),
            device_id_type=pl.DeviceIdType.MESH,
        )

    def arrived(slot):
        remote(slot, slot, z_sem, sibling).wait_recv()

    def to_sibling(i):
        return remote(2 * i + 2 - 2 * core, 2 * i + 1, pair_sem.at[i], sibling)

    def sibling_wants(i):
        return 2 * chip + 2 * i + 2 - 2 * core < devices

    def z_copy():
        return remote(0, far, z_sem, me - 2 * per_layer)

    def layer_copy(d, source):
        return remote(source, 2 * d, layer_sem.at[d - 1], in_layer(d))

    def ten_copy():
        return remote(far, last, ten_sem, me - 2)

    @pl.when(has_down)
    def _():
        z_copy().start()

    for d in range(per_layer - 1, 0, -1):
        @pl.when(place >= d)
        def _(d=d):
            layer_copy(d, 0).start()

    @pl.when(core == 1)
    def _():
        to_sibling(0).start()

    padded = jnp.concatenate(
        [own.astype(jnp.float32), jnp.zeros((events, LANES), jnp.float32)], axis=1
    )
    width = samples + LANES
    for lag in range(LAGS):
        moved = pltpu.roll(padded, (lag - HALF) % width, 1) if lag != HALF else padded
        shifted[lag] = moved[:, :samples].astype(jnp.bfloat16)
    ones = jnp.ones((samples, LANES), jnp.bfloat16)
    high, low = split_squares(own)
    row_scale[...] = lax.rsqrt(
        lax.dot_general(high, ones, NN, preferred_element_type=jnp.float32)
        + lax.dot_general(low, ones, NN, preferred_element_type=jnp.float32)
        + epsilon
    )

    def pass_far():
        @pl.when(has_up)
        def _():
            arrived(far)
            for d in range(per_layer - 1, 0, -1):
                @pl.when(place < d)
                def _(d=d):
                    layer_copy(d, far).start()

            @pl.when((core == 0) & (chip >= 1))
            def _():
                ten_copy().start()

            @pl.when(core == 0)
            def _():
                to_sibling(far // 2 - 1).start()

            @pl.when(core == 1)
            def _():
                to_sibling(far // 2).start()

    def pass_on(slot):
        @pl.when(2 * chip + slot < devices)
        def _():
            arrived(slot)

            @pl.when(core == 0)
            def _():
                to_sibling(slot // 2 - 1).start()

            @pl.when(core == 1)
            def _():
                to_sibling(slot // 2).start()

    def pass_last():
        @pl.when((core == 0) & (me + last < devices))
        def _():
            arrived(last)
            to_sibling(last // 2 - 1).start()

    def receive(slot):
        @pl.when(me + slot < devices)
        def _():
            arrived(slot)

    def correlate(slots):
        for i, slot in enumerate(slots):
            high, low = split_squares(held[slot])
            rows = jnp.ones((8, samples), jnp.bfloat16)
            total = lax.dot_general(rows, high, NT, preferred_element_type=jnp.float32)
            total += lax.dot_general(rows, low, NT, preferred_element_type=jnp.float32)
            partner_scale = lax.rsqrt(total + epsilon)
            if slot > 0:
                partner_scale *= pair_valid[0, slot - 1].astype(jnp.float32)
            scale[:, i * events : (i + 1) * events] = row_scale[...] * partner_scale[0:1, :]

        def some_lags(c, carry):
            lags = pl.ds(c * LAGS_AT_ONCE, LAGS_AT_ONCE)
            left = shifted[lags].reshape(LAGS_AT_ONCE * events, samples)
            right = jnp.concatenate([held[slot] for slot in slots], axis=0)
            product = lax.dot_general(left, right, NT, preferred_element_type=jnp.float32)
            product = product.reshape(LAGS_AT_ONCE, events, len(slots) * events)
            product = (product * scale[...][None]).astype(jnp.bfloat16)
            for i, slot in enumerate(slots):
                out[slot, lags] = product[:, :, i * events : (i + 1) * events]
            return carry

        lax.fori_loop(0, LAGS // LAGS_AT_ONCE, some_lags, 0)

    pass_far()
    correlate((0, far))
    evens = list(range(2, far, 2))
    ready = []
    for slot in evens:
        pass_on(slot)
        ready.append(slot)
        if len(ready) == 2:
            correlate(tuple(ready))
            ready = []
    pass_last()
    for slot in range(1, reach + 1, 2):
        receive(slot)
        ready.append(slot)
        if len(ready) == 2:
            correlate(tuple(ready))
            ready = []

    @pl.when(has_down)
    def _():
        z_copy().wait_send()

    for d in range(1, per_layer):
        @pl.when((place >= d) | has_up)
        def _(d=d):
            layer_copy(d, 0).wait_send()

    @pl.when((core == 0) & (chip >= 1) & has_up)
    def _():
        ten_copy().wait_send()

    for i in range((reach + 1) // 2):
        @pl.when(sibling_wants(i))
        def _(i=i):
            to_sibling(i).wait_send()


def shards(devices, records, filter_taps, live_counts, pair_valid):
    events, samples = records.shape
    reach = pair_valid.shape[1]
    vmem = pl.BlockSpec(memory_space=pltpu.VMEM)
    smem = pl.BlockSpec(memory_space=pltpu.SMEM)
    correlations = pl.pallas_call(
        functools.partial(kernel, devices),
        out_shape=pltpu.VMEM((reach + 1, LAGS, events, events), jnp.bfloat16),
        in_specs=[vmem, vmem, smem, smem],
        out_specs=vmem,
        scratch_shapes=[
            pltpu.VMEM((reach + 2, events, samples), jnp.bfloat16),
            pltpu.VMEM((LAGS, events, samples), jnp.bfloat16),
            pltpu.VMEM((8, samples), jnp.float32),
            pltpu.VMEM((events, LANES), jnp.float32),
            pltpu.VMEM((events, 2 * events), jnp.float32),
            pltpu.SemaphoreType.DMA,
            pltpu.SemaphoreType.DMA(((reach - 1) // 2 - 1,)),
            pltpu.SemaphoreType.DMA,
            pltpu.SemaphoreType.DMA(((reach + 1) // 2,)),
            pltpu.SemaphoreType.DMA((reach + 2,)),
        ],
        compiler_params=pltpu.CompilerParams(
            collective_id=0, has_side_effects=True, vmem_limit_bytes=40 * 1024 * 1024
        ),
        cost_estimate=pl.CostEstimate(
            flops=2 * (reach + 1) * LAGS * events * events * samples,
            bytes_accessed=2 * (reach + 1) * LAGS * events * events,
            transcendentals=0,
        ),
    )(records, filter_taps.reshape(1, -1), live_counts, pair_valid)
    return jnp.transpose(correlations, (2, 0, 1, 3))


def solution(mesh):
    in_specs = (P("ev", None), P(), P("ev"), P("ev", None))
    out_specs = P("ev", None, None, None)
    return jax.shard_map(
        functools.partial(shards, mesh.shape["ev"]),
        mesh=mesh, in_specs=in_specs, out_specs=out_specs, check_vma=False,
    )
```

```python
import functools

import jax
import jax.numpy as jnp
from jax import lax
from jax.experimental import pallas as pl
from jax.experimental.pallas import tpu as pltpu
from jax.sharding import PartitionSpec as P

HALF = 12
LAGS = 2 * HALF + 1
PARTS = 2
LANES = 128

epsilon = 1e-06

NT = (((1,), (1,)), ((), ()))
NN = (((1,), (0,)), ((), ()))


def split_squares(block):
    wide = block.astype(jnp.float32)
    square = wide * wide
    high = square.astype(jnp.bfloat16)
    low = (square - high.astype(jnp.float32)).astype(jnp.bfloat16)
    return high, low


def kernel(
    devices, records_in, taps_in, live_count, pair_valid_in, out,
    records, taps, pair_valid,
    held, shifted, spread, row_scale, scale,
    in_sem, z_sem, layer_sem, ten_sem, pair_sem, recv_sem,
):
    events, samples = records.shape
    reach = pair_valid.shape[1]
    half_taps = (taps.shape[1] - 1) // 2
    per_layer = (reach - 1) // 2
    far = reach - 1
    last = reach + 1
    chips = devices // 2
    me = lax.axis_index("ev")
    core = lax.rem(me, 2)
    chip = me // 2
    place = lax.rem(chip, per_layer)
    sibling = me + 1 - 2 * core

    def in_layer(d):
        return me - 2 * place + 2 * lax.rem(place + per_layer - d, per_layer)

    barrier = pltpu.get_barrier_semaphore()

    def greet(device):
        pl.semaphore_signal(
            barrier, inc=1, device_id=(device,), device_id_type=pl.DeviceIdType.MESH
        )

    inputs = [
        pltpu.make_async_copy(there, here, in_sem.at[i])
        for i, (there, here) in enumerate(
            [
                (taps_in, taps),
                (records_in, records),
                (pair_valid_in, pair_valid),
            ]
        )
    ]
    for copy in inputs:
        copy.start()

    has_down = chip >= per_layer
    has_up = chip + per_layer < chips
    across = {}
    for d in range(1, per_layer, 2):
        across[d] = (
            (place == d // 2) & has_down,
            (place == per_layer - 1 - d // 2) & (chip + d < chips),
        )
    greet(sibling)
    greeted = per_layer + has_down.astype(jnp.int32) + has_up.astype(jnp.int32)
    for d in range(1, per_layer):
        greet(in_layer(d))

    @pl.when(has_down)
    def _():
        greet(me - 2 * per_layer)

    @pl.when(has_up)
    def _():
        greet(me + 2 * per_layer)

    for d, (down, up) in across.items():
        greeted += down.astype(jnp.int32) + up.astype(jnp.int32)

        @pl.when(down)
        def _(d=d):
            greet(me - 2 * d)

        @pl.when(up)
        def _(d=d):
            greet(me + 2 * d)

    spread[...] = jnp.zeros_like(spread)
    inputs[0].wait()
    spread[0:1, 0 : taps.shape[1]] = taps[...].astype(jnp.float32)
    rolled = pltpu.roll(
        jnp.broadcast_to(spread[0:1, :], (samples, samples)),
        samples - half_taps, 1, stride=1, stride_axis=0,
    )
    t = lax.broadcasted_iota(jnp.int32, (samples, samples), 0)
    u = lax.broadcasted_iota(jnp.int32, (samples, samples), 1)
    band = jnp.where(jnp.abs(u - t) <= half_taps, rolled, 0.0).astype(jnp.bfloat16)
    row = lax.broadcasted_iota(jnp.int32, (events, samples), 0)
    inputs[1].wait()
    kept = jnp.where(row < live_count[0], records[...].astype(jnp.float32), 0.0)
    own = lax.dot_general(
        kept.astype(jnp.bfloat16), band, NT, preferred_element_type=jnp.float32
    ).astype(jnp.bfloat16)
    held[0] = own

    for k in range(1, last + 1):
        if k == last:
            missing = (core == 0) & (me + k >= devices)
        else:
            missing = me + k >= devices

        @pl.when(missing)
        def _(k=k):
            held[k] = jnp.zeros((events, samples), jnp.bfloat16)

    pl.semaphore_wait(barrier, greeted)

    def remote(source, slot, send_sem, device, part=None):
        rows = pl.ds(0, events)
        if part is not None:
            rows = pl.ds(part * (events // PARTS), events // PARTS)
        return pltpu.make_async_remote_copy(
            src_ref=held.at[source, rows],
            dst_ref=held.at[slot, rows],
            send_sem=send_sem,
            recv_sem=recv_sem.at[slot, part or 0],
            device_id=(device,),
            device_id_type=pl.DeviceIdType.MESH,
        )

    def arrived(slot, part):
        remote(slot, slot, z_sem.at[part or 0], sibling, part).wait_recv()

    def to_sibling(i):
        return remote(2 * i + 2 - 2 * core, 2 * i + 1, pair_sem.at[i], sibling)

    def sibling_wants(i):
        return 2 * chip + 2 * i + 2 - 2 * core < devices

    def z_copy(part):
        return remote(0, far, z_sem.at[part], me - 2 * per_layer, part)

    def across_copy(d, part):
        return remote(0, 2 * d, layer_sem.at[d - 1, part], me - 2 * d, part)

    def layer_copy(d, source, part):
        return remote(source, 2 * d, layer_sem.at[d - 1, part], in_layer(d), part)

    def relays(d):
        return has_up & (place < d) & (d != 2 * place + 1)

    def ten_copy(part):
        return remote(far, last, ten_sem.at[part], me - 2, part)

    @pl.when(has_down)
    def _():
        for part in range(PARTS):
            z_copy(part).start()

    for d, (down, up) in across.items():
        @pl.when(down)
        def _(d=d):
            for part in range(PARTS):
                across_copy(d, part).start()

    for d in range(per_layer - 1, 0, -1):
        @pl.when(place >= d)
        def _(d=d):
            for part in range(PARTS):
                layer_copy(d, 0, part).start()

    @pl.when(core == 1)
    def _():
        to_sibling(0).start()

    padded = jnp.concatenate(
        [own.astype(jnp.float32), jnp.zeros((events, LANES), jnp.float32)], axis=1
    )
    width = samples + LANES
    for lag in range(LAGS):
        moved = pltpu.roll(padded, (lag - HALF) % width, 1) if lag != HALF else padded
        shifted[lag] = moved[:, :samples].astype(jnp.bfloat16)
    ones = jnp.ones((samples, LANES), jnp.bfloat16)
    high, low = split_squares(own)
    row_scale[...] = lax.rsqrt(
        lax.dot_general(high, ones, NN, preferred_element_type=jnp.float32)
        + lax.dot_general(low, ones, NN, preferred_element_type=jnp.float32)
        + epsilon
    )

    def pass_far():
        for part in range(PARTS):
            @pl.when(has_up)
            def _(part=part):
                arrived(far, part)

            for d in range(per_layer - 1, 0, -1):
                @pl.when(relays(d))
                def _(d=d, part=part):
                    layer_copy(d, far, part).start()

            @pl.when((core == 0) & (chip >= 1) & has_up)
            def _(part=part):
                ten_copy(part).start()

        @pl.when((core == 0) & has_up)
        def _():
            to_sibling(far // 2 - 1).start()

        @pl.when((core == 1) & has_up)
        def _():
            to_sibling(far // 2).start()

    def pass_on(slot):
        @pl.when(2 * chip + slot < devices)
        def _():
            for part in range(PARTS):
                arrived(slot, part)

            @pl.when(core == 0)
            def _():
                to_sibling(slot // 2 - 1).start()

            @pl.when(core == 1)
            def _():
                to_sibling(slot // 2).start()

    def pass_last():
        @pl.when((core == 0) & (me + last < devices))
        def _():
            for part in range(PARTS):
                arrived(last, part)
            to_sibling(last // 2 - 1).start()

    def receive(slot):
        @pl.when(me + slot < devices)
        def _():
            arrived(slot, None)

    def correlate(slots):
        for i, slot in enumerate(slots):
            high, low = split_squares(held[slot])
            rows = jnp.ones((8, samples), jnp.bfloat16)
            total = lax.dot_general(rows, high, NT, preferred_element_type=jnp.float32)
            total += lax.dot_general(rows, low, NT, preferred_element_type=jnp.float32)
            partner_scale = lax.rsqrt(total + epsilon)
            if slot > 0:
                partner_scale *= pair_valid[0, slot - 1].astype(jnp.float32)
            scale[:, i * events : (i + 1) * events] = row_scale[...] * partner_scale[0:1, :]

        left = shifted[...].reshape(LAGS * events, samples)
        right = jnp.concatenate([held[slot] for slot in slots], axis=0)
        product = lax.dot_general(left, right, NT, preferred_element_type=jnp.float32)
        product = product.reshape(LAGS, events, len(slots) * events)
        product = (product * scale[...][None]).astype(jnp.bfloat16)
        for i, slot in enumerate(slots):
            out[slot] = product[:, :, i * events : (i + 1) * events]

    inputs[2].wait()
    pass_far()
    correlate((0, far))
    evens = list(range(2, far, 2))
    ready = []
    for slot in evens:
        pass_on(slot)
        ready.append(slot)
        if len(ready) == 2:
            correlate(tuple(ready))
            ready = []
    pass_last()
    for slot in range(1, reach + 1, 2):
        receive(slot)
        ready.append(slot)
        if len(ready) == 2:
            correlate(tuple(ready))
            ready = []

    for part in range(PARTS):
        @pl.when(has_down)
        def _(part=part):
            z_copy(part).wait_send()

        for d in range(1, per_layer):
            @pl.when((place >= d) | relays(d))
            def _(d=d, part=part):
                layer_copy(d, 0, part).wait_send()

        for d, (down, up) in across.items():
            @pl.when(down)
            def _(d=d, part=part):
                across_copy(d, part).wait_send()

        @pl.when((core == 0) & (chip >= 1) & has_up)
        def _(part=part):
            ten_copy(part).wait_send()

    for i in range((reach + 1) // 2):
        @pl.when(sibling_wants(i))
        def _(i=i):
            to_sibling(i).wait_send()


def shards(devices, records, filter_taps, live_counts, pair_valid):
    events, samples = records.shape
    reach = pair_valid.shape[1]
    vmem = pl.BlockSpec(memory_space=pltpu.VMEM)
    hbm = pl.BlockSpec(memory_space=pltpu.HBM)
    taps = filter_taps.reshape(1, -1)
    records, taps, pair_valid = [
        pltpu.with_memory_space_constraint(x, pltpu.HBM)
        for x in (records, taps, pair_valid)
    ]
    correlations = pl.pallas_call(
        functools.partial(kernel, devices),
        out_shape=pltpu.VMEM((reach + 1, LAGS, events, events), jnp.bfloat16),
        in_specs=[hbm, hbm, pl.BlockSpec(memory_space=pltpu.SMEM), hbm],
        out_specs=vmem,
        scratch_shapes=[
            pltpu.VMEM((events, samples), jnp.bfloat16),
            pltpu.VMEM((1, filter_taps.shape[0]), jnp.bfloat16),
            pltpu.SMEM((1, reach), jnp.int32),
            pltpu.VMEM((reach + 2, events, samples), jnp.bfloat16),
            pltpu.VMEM((LAGS, events, samples), jnp.bfloat16),
            pltpu.VMEM((8, samples), jnp.float32),
            pltpu.VMEM((events, LANES), jnp.float32),
            pltpu.VMEM((events, 2 * events), jnp.float32),
            pltpu.SemaphoreType.DMA((3,)),
            pltpu.SemaphoreType.DMA((PARTS,)),
            pltpu.SemaphoreType.DMA(((reach - 1) // 2 - 1, PARTS)),
            pltpu.SemaphoreType.DMA((PARTS,)),
            pltpu.SemaphoreType.DMA(((reach + 1) // 2,)),
            pltpu.SemaphoreType.DMA((reach + 2, PARTS)),
        ],
        compiler_params=pltpu.CompilerParams(
            collective_id=0, has_side_effects=True, vmem_limit_bytes=40 * 1024 * 1024
        ),
        cost_estimate=pl.CostEstimate(
            flops=2 * (reach + 1) * LAGS * events * events * samples,
            bytes_accessed=2 * (reach + 1) * LAGS * events * events,
            transcendentals=0,
        ),
    )(records, taps, live_counts, pair_valid)
    return jnp.transpose(correlations, (2, 0, 1, 3))


def solution(mesh):
    in_specs = (P("ev", None), P(), P("ev"), P("ev", None))
    out_specs = P("ev", None, None, None)
    return jax.shard_map(
        functools.partial(shards, mesh.shape["ev"]),
        mesh=mesh, in_specs=in_specs, out_specs=out_specs, check_vma=False,
    )
```

```python
import functools

import jax
import jax.numpy as jnp
from jax import lax
from jax.experimental import pallas as pl
from jax.experimental.pallas import tpu as pltpu
from jax.sharding import PartitionSpec as P

HALF = 12
LAGS = 2 * HALF + 1
PARTS = 2
LANES = 128

epsilon = 1e-06

NT = (((1,), (1,)), ((), ()))
NN = (((1,), (0,)), ((), ()))


def split_squares(block):
    wide = block.astype(jnp.float32)
    square = wide * wide
    high = square.astype(jnp.bfloat16)
    low = (square - high.astype(jnp.float32)).astype(jnp.bfloat16)
    return high, low


def in_order(reach):
    order = [0, reach - 1, *range(2, reach - 1, 2), *range(1, reach + 1, 2)]
    pairs = [tuple(order[i : i + 2]) for i in range(0, len(order), 2)]
    return pairs[:-2], pairs[-2:]


def product_of(shifted, right, scale):
    lags, events, samples = shifted.shape
    left = shifted[...].reshape(lags * events, samples)
    product = lax.dot_general(left, right, NT, preferred_element_type=jnp.float32)
    return (product.reshape(lags, events, -1) * scale[None]).astype(jnp.bfloat16)


def finish(first, second, done, shifted, late, late_scale, out, fresh, sems):
    events = shifted.shape[1]
    copies = []

    def send(source, slot):
        copy = pltpu.make_async_copy(source, out.at[slot], sems.at[len(copies)])
        copy.start()
        copies.append(copy)

    for n, slot in enumerate(sum(first, ())):
        send(done.at[n], slot)
    n = 0
    for i, slots in enumerate(second):
        right = late[n : n + len(slots)].reshape(len(slots) * events, -1)
        product = product_of(shifted, right, late_scale[i])
        for j, slot in enumerate(slots):
            fresh[n] = product[:, :, j * events : (j + 1) * events]
            send(fresh.at[n], slot)
            n += 1
    for copy in copies:
        copy.wait()


def kernel(
    devices, records_in, taps_in, live_count, pair_valid_in,
    done, shifted, late, late_scale,
    records, taps, pair_valid,
    held, spread, row_scale,
    in_sem, z_sem, layer_sem, ten_sem, pair_sem, recv_sem,
):
    events, samples = records.shape
    reach = pair_valid.shape[1]
    half_taps = (taps.shape[1] - 1) // 2
    per_layer = (reach - 1) // 2
    far = reach - 1
    last = reach + 1
    chips = devices // 2
    me = lax.axis_index("ev")
    core = lax.rem(me, 2)
    chip = me // 2
    place = lax.rem(chip, per_layer)
    sibling = me + 1 - 2 * core

    def in_layer(d):
        return me - 2 * place + 2 * lax.rem(place + per_layer - d, per_layer)

    barrier = pltpu.get_barrier_semaphore()

    def greet(device):
        pl.semaphore_signal(
            barrier, inc=1, device_id=(device,), device_id_type=pl.DeviceIdType.MESH
        )

    inputs = [
        pltpu.make_async_copy(there, here, in_sem.at[i])
        for i, (there, here) in enumerate(
            [
                (taps_in, taps),
                (records_in, records),
                (pair_valid_in, pair_valid),
            ]
        )
    ]
    for copy in inputs:
        copy.start()

    has_down = chip >= per_layer
    has_up = chip + per_layer < chips
    across = {}
    for d in range(1, per_layer, 2):
        across[d] = (
            (place == d // 2) & has_down,
            (place == per_layer - 1 - d // 2) & (chip + d < chips),
        )
    greet(sibling)
    greeted = per_layer + has_down.astype(jnp.int32) + has_up.astype(jnp.int32)
    for d in range(1, per_layer):
        greet(in_layer(d))

    @pl.when(has_down)
    def _():
        greet(me - 2 * per_layer)

    @pl.when(has_up)
    def _():
        greet(me + 2 * per_layer)

    for d, (down, up) in across.items():
        greeted += down.astype(jnp.int32) + up.astype(jnp.int32)

        @pl.when(down)
        def _(d=d):
            greet(me - 2 * d)

        @pl.when(up)
        def _(d=d):
            greet(me + 2 * d)

    spread[...] = jnp.zeros_like(spread)
    inputs[0].wait()
    spread[0:1, 0 : taps.shape[1]] = taps[...].astype(jnp.float32)
    rolled = pltpu.roll(
        jnp.broadcast_to(spread[0:1, :], (samples, samples)),
        samples - half_taps, 1, stride=1, stride_axis=0,
    )
    t = lax.broadcasted_iota(jnp.int32, (samples, samples), 0)
    u = lax.broadcasted_iota(jnp.int32, (samples, samples), 1)
    band = jnp.where(jnp.abs(u - t) <= half_taps, rolled, 0.0).astype(jnp.bfloat16)
    row = lax.broadcasted_iota(jnp.int32, (events, samples), 0)
    inputs[1].wait()
    kept = jnp.where(row < live_count[0], records[...].astype(jnp.float32), 0.0)
    own = lax.dot_general(
        kept.astype(jnp.bfloat16), band, NT, preferred_element_type=jnp.float32
    ).astype(jnp.bfloat16)
    held[0] = own

    for k in range(1, last + 1):
        if k == last:
            missing = (core == 0) & (me + k >= devices)
        else:
            missing = me + k >= devices

        @pl.when(missing)
        def _(k=k):
            held[k] = jnp.zeros((events, samples), jnp.bfloat16)

    pl.semaphore_wait(barrier, greeted)

    def remote(source, slot, send_sem, device, part=None):
        rows = pl.ds(0, events)
        if part is not None:
            rows = pl.ds(part * (events // PARTS), events // PARTS)
        return pltpu.make_async_remote_copy(
            src_ref=held.at[source, rows],
            dst_ref=held.at[slot, rows],
            send_sem=send_sem,
            recv_sem=recv_sem.at[slot, part or 0],
            device_id=(device,),
            device_id_type=pl.DeviceIdType.MESH,
        )

    def arrived(slot, part):
        remote(slot, slot, z_sem.at[part or 0], sibling, part).wait_recv()

    def to_sibling(i):
        return remote(2 * i + 2 - 2 * core, 2 * i + 1, pair_sem.at[i], sibling)

    def sibling_wants(i):
        return 2 * chip + 2 * i + 2 - 2 * core < devices

    def z_copy(part):
        return remote(0, far, z_sem.at[part], me - 2 * per_layer, part)

    def across_copy(d, part):
        return remote(0, 2 * d, layer_sem.at[d - 1, part], me - 2 * d, part)

    def layer_copy(d, source, part):
        return remote(source, 2 * d, layer_sem.at[d - 1, part], in_layer(d), part)

    def relays(d):
        return has_up & (place < d) & (d != 2 * place + 1)

    def ten_copy(part):
        return remote(far, last, ten_sem.at[part], me - 2, part)

    @pl.when(has_down)
    def _():
        for part in range(PARTS):
            z_copy(part).start()

    for d, (down, up) in across.items():
        @pl.when(down)
        def _(d=d):
            for part in range(PARTS):
                across_copy(d, part).start()

    for d in range(per_layer - 1, 0, -1):
        @pl.when(place >= d)
        def _(d=d):
            for part in range(PARTS):
                layer_copy(d, 0, part).start()

    @pl.when(core == 1)
    def _():
        to_sibling(0).start()

    padded = jnp.concatenate(
        [own.astype(jnp.float32), jnp.zeros((events, LANES), jnp.float32)], axis=1
    )
    width = samples + LANES
    for lag in range(LAGS):
        moved = pltpu.roll(padded, (lag - HALF) % width, 1) if lag != HALF else padded
        shifted[lag] = moved[:, :samples].astype(jnp.bfloat16)
    ones = jnp.ones((samples, LANES), jnp.bfloat16)
    high, low = split_squares(own)
    row_scale[...] = lax.rsqrt(
        lax.dot_general(high, ones, NN, preferred_element_type=jnp.float32)
        + lax.dot_general(low, ones, NN, preferred_element_type=jnp.float32)
        + epsilon
    )

    def pass_far():
        for part in range(PARTS):
            @pl.when(has_up)
            def _(part=part):
                arrived(far, part)

            for d in range(per_layer - 1, 0, -1):
                @pl.when(relays(d))
                def _(d=d, part=part):
                    layer_copy(d, far, part).start()

            @pl.when((core == 0) & (chip >= 1) & has_up)
            def _(part=part):
                ten_copy(part).start()

        @pl.when((core == 0) & has_up)
        def _():
            to_sibling(far // 2 - 1).start()

        @pl.when((core == 1) & has_up)
        def _():
            to_sibling(far // 2).start()

    def pass_on(slot):
        @pl.when(2 * chip + slot < devices)
        def _():
            for part in range(PARTS):
                arrived(slot, part)

            @pl.when(core == 0)
            def _():
                to_sibling(slot // 2 - 1).start()

            @pl.when(core == 1)
            def _():
                to_sibling(slot // 2).start()

    def pass_last():
        @pl.when((core == 0) & (me + last < devices))
        def _():
            for part in range(PARTS):
                arrived(last, part)
            to_sibling(last // 2 - 1).start()

    def receive(slot):
        @pl.when(me + slot < devices)
        def _():
            arrived(slot, None)

    def scale_of(slots):
        parts = []
        for slot in slots:
            high, low = split_squares(held[slot])
            rows = jnp.ones((8, samples), jnp.bfloat16)
            total = lax.dot_general(rows, high, NT, preferred_element_type=jnp.float32)
            total += lax.dot_general(rows, low, NT, preferred_element_type=jnp.float32)
            partner_scale = lax.rsqrt(total + epsilon)
            if slot > 0:
                partner_scale *= pair_valid[0, slot - 1].astype(jnp.float32)
            parts.append(row_scale[...] * partner_scale[0:1, :])
        return jnp.concatenate(parts, axis=1)

    first, second = in_order(reach)
    inputs[2].wait()

    def await_slot(slot):
        if slot == 0:
            return
        if slot == far:
            pass_far()
        elif slot % 2 == 0:
            pass_on(slot)
            if slot == far - 2:
                pass_last()
        else:
            receive(slot)

    n = 0
    for slots in first:
        for slot in slots:
            await_slot(slot)
        right = jnp.concatenate([held[slot] for slot in slots], axis=0)
        product = product_of(shifted, right, scale_of(slots))
        for i in range(len(slots)):
            done[n] = product[:, :, i * events : (i + 1) * events]
            n += 1
    n = 0
    for i, slots in enumerate(second):
        for slot in slots:
            await_slot(slot)
            late[n] = held[slot]
            n += 1
        late_scale[i] = scale_of(slots)

    for part in range(PARTS):
        @pl.when(has_down)
        def _(part=part):
            z_copy(part).wait_send()

        for d in range(1, per_layer):
            @pl.when((place >= d) | relays(d))
            def _(d=d, part=part):
                layer_copy(d, 0, part).wait_send()

        for d, (down, up) in across.items():
            @pl.when(down)
            def _(d=d, part=part):
                across_copy(d, part).wait_send()

        @pl.when((core == 0) & (chip >= 1) & has_up)
        def _(part=part):
            ten_copy(part).wait_send()

    for i in range((reach + 1) // 2):
        @pl.when(sibling_wants(i))
        def _(i=i):
            to_sibling(i).wait_send()


def shards(devices, records, filter_taps, live_counts, pair_valid):
    events, samples = records.shape
    reach = pair_valid.shape[1]
    vmem = pl.BlockSpec(memory_space=pltpu.VMEM)
    hbm = pl.BlockSpec(memory_space=pltpu.HBM)
    taps = filter_taps.reshape(1, -1)
    records, taps, pair_valid = [
        pltpu.with_memory_space_constraint(x, pltpu.HBM)
        for x in (records, taps, pair_valid)
    ]
    first, second = in_order(reach)
    done_count = sum(len(slots) for slots in first)
    late_count = sum(len(slots) for slots in second)
    arrays = pl.pallas_call(
        functools.partial(kernel, devices),
        out_shape=[
            pltpu.VMEM((done_count, LAGS, events, events), jnp.bfloat16),
            pltpu.VMEM((LAGS, events, samples), jnp.bfloat16),
            pltpu.VMEM((late_count, events, samples), jnp.bfloat16),
            pltpu.VMEM((len(second), events, 2 * events), jnp.float32),
        ],
        in_specs=[hbm, hbm, pl.BlockSpec(memory_space=pltpu.SMEM), hbm],
        out_specs=[vmem] * 4,
        scratch_shapes=[
            pltpu.VMEM((events, samples), jnp.bfloat16),
            pltpu.VMEM((1, filter_taps.shape[0]), jnp.bfloat16),
            pltpu.SMEM((1, reach), jnp.int32),
            pltpu.VMEM((reach + 2, events, samples), jnp.bfloat16),
            pltpu.VMEM((8, samples), jnp.float32),
            pltpu.VMEM((events, LANES), jnp.float32),
            pltpu.SemaphoreType.DMA((3,)),
            pltpu.SemaphoreType.DMA((PARTS,)),
            pltpu.SemaphoreType.DMA(((reach - 1) // 2 - 1, PARTS)),
            pltpu.SemaphoreType.DMA((PARTS,)),
            pltpu.SemaphoreType.DMA(((reach + 1) // 2,)),
            pltpu.SemaphoreType.DMA((reach + 2, PARTS)),
        ],
        compiler_params=pltpu.CompilerParams(
            collective_id=0, has_side_effects=True, vmem_limit_bytes=24 * 1024 * 1024
        ),
        cost_estimate=pl.CostEstimate(
            flops=2 * (reach + 1) * LAGS * events * events * samples,
            bytes_accessed=2 * (reach + 1) * LAGS * events * events,
            transcendentals=0,
        ),
    )(records, taps, live_counts, pair_valid)
    correlations = pl.pallas_call(
        functools.partial(finish, first, second),
        out_shape=jax.ShapeDtypeStruct((reach + 1, LAGS, events, events), jnp.bfloat16),
        in_specs=[vmem] * 4,
        out_specs=hbm,
        scratch_shapes=[
            pltpu.VMEM((late_count, LAGS, events, events), jnp.bfloat16),
            pltpu.SemaphoreType.DMA((reach + 1,)),
        ],
        compiler_params=pltpu.CompilerParams(vmem_limit_bytes=24 * 1024 * 1024),
    )(*arrays)
    return jnp.transpose(correlations, (2, 0, 1, 3))


def solution(mesh):
    in_specs = (P("ev", None), P(), P("ev"), P("ev", None))
    out_specs = P("ev", None, None, None)
    return jax.shard_map(
        functools.partial(shards, mesh.shape["ev"]),
        mesh=mesh, in_specs=in_specs, out_specs=out_specs, check_vma=False,
    )
```

```python
import functools

import jax
import jax.numpy as jnp
from jax import lax
from jax.experimental import pallas as pl
from jax.experimental.pallas import tpu as pltpu
from jax.sharding import PartitionSpec as P

HALF = 12
LAGS = 2 * HALF + 1
PARTS = 4
LANES = 128

epsilon = 1e-06

NT = (((1,), (1,)), ((), ()))
NN = (((1,), (0,)), ((), ()))


def split_squares(block):
    wide = block.astype(jnp.float32)
    square = wide * wide
    high = square.astype(jnp.bfloat16)
    low = (square - high.astype(jnp.float32)).astype(jnp.bfloat16)
    return high, low


def in_order(reach):
    order = [0, reach - 1, *range(2, reach - 1, 2), *range(1, reach + 1, 2)]
    pairs = [tuple(order[i : i + 2]) for i in range(0, len(order), 2)]
    return pairs[:-2], pairs[-2:]


def product_of(shifted, right, scale):
    lags, events, samples = shifted.shape
    left = shifted[...].reshape(lags * events, samples)
    product = lax.dot_general(left, right, NT, preferred_element_type=jnp.float32)
    return (product.reshape(lags, events, -1) * scale[None]).astype(jnp.bfloat16)


def finish(first, second, done, shifted, late, late_scale, out, fresh, sems):
    events = shifted.shape[1]
    copies = []

    def send(source, slot):
        copy = pltpu.make_async_copy(source, out.at[slot], sems.at[len(copies)])
        copy.start()
        copies.append(copy)

    for n, slot in enumerate(sum(first, ())):
        send(done.at[n], slot)
    n = 0
    for i, slots in enumerate(second):
        right = late[n : n + len(slots)].reshape(len(slots) * events, -1)
        product = product_of(shifted, right, late_scale[i])
        for j, slot in enumerate(slots):
            fresh[n] = product[:, :, j * events : (j + 1) * events]
            send(fresh.at[n], slot)
            n += 1
    for copy in copies:
        copy.wait()


def kernel(
    devices, records_in, taps_in, live_count, pair_valid_in,
    done, shifted, late, late_scale,
    records, taps, pair_valid,
    held, spread, row_scale,
    in_sem, z_sem, layer_sem, ten_sem, pair_sem, recv_sem,
):
    events, samples = records.shape
    reach = pair_valid.shape[1]
    half_taps = (taps.shape[1] - 1) // 2
    per_layer = (reach - 1) // 2
    far = reach - 1
    last = reach + 1
    chips = devices // 2
    me = lax.axis_index("ev")
    core = lax.rem(me, 2)
    chip = me // 2
    place = lax.rem(chip, per_layer)
    sibling = me + 1 - 2 * core

    def in_layer(d):
        return me - 2 * place + 2 * lax.rem(place + per_layer - d, per_layer)

    barrier = pltpu.get_barrier_semaphore()

    def greet(device):
        pl.semaphore_signal(
            barrier, inc=1, device_id=(device,), device_id_type=pl.DeviceIdType.MESH
        )

    inputs = [
        pltpu.make_async_copy(there, here, in_sem.at[i])
        for i, (there, here) in enumerate(
            [
                (taps_in, taps),
                (records_in, records),
                (pair_valid_in, pair_valid),
            ]
        )
    ]
    for copy in inputs:
        copy.start()

    has_down = chip >= per_layer
    has_up = chip + per_layer < chips
    across = {}
    for d in range(1, per_layer, 2):
        across[d] = (
            (place == d // 2) & has_down,
            (place == per_layer - 1 - d // 2) & (chip + d < chips),
        )
    greet(sibling)
    greeted = per_layer + has_down.astype(jnp.int32) + has_up.astype(jnp.int32)
    for d in range(1, per_layer):
        greet(in_layer(d))

    @pl.when(has_down)
    def _():
        greet(me - 2 * per_layer)

    @pl.when(has_up)
    def _():
        greet(me + 2 * per_layer)

    for d, (down, up) in across.items():
        greeted += down.astype(jnp.int32) + up.astype(jnp.int32)

        @pl.when(down)
        def _(d=d):
            greet(me - 2 * d)

        @pl.when(up)
        def _(d=d):
            greet(me + 2 * d)

    spread[...] = jnp.zeros_like(spread)
    inputs[0].wait()
    spread[0:1, 0 : taps.shape[1]] = taps[...].astype(jnp.float32)
    rolled = pltpu.roll(
        jnp.broadcast_to(spread[0:1, :], (samples, samples)),
        samples - half_taps, 1, stride=1, stride_axis=0,
    )
    t = lax.broadcasted_iota(jnp.int32, (samples, samples), 0)
    u = lax.broadcasted_iota(jnp.int32, (samples, samples), 1)
    band = jnp.where(jnp.abs(u - t) <= half_taps, rolled, 0.0).astype(jnp.bfloat16)
    row = lax.broadcasted_iota(jnp.int32, (events, samples), 0)
    inputs[1].wait()
    kept = jnp.where(row < live_count[0], records[...].astype(jnp.float32), 0.0)
    own = lax.dot_general(
        kept.astype(jnp.bfloat16), band, NT, preferred_element_type=jnp.float32
    ).astype(jnp.bfloat16)
    held[0] = own

    for k in range(1, last + 1):
        if k == last:
            missing = (core == 0) & (me + k >= devices)
        else:
            missing = me + k >= devices

        @pl.when(missing)
        def _(k=k):
            held[k] = jnp.zeros((events, samples), jnp.bfloat16)

    pl.semaphore_wait(barrier, greeted)

    def remote(source, slot, send_sem, device, part=None):
        rows = pl.ds(0, events)
        if part is not None:
            rows = pl.ds(part * (events // PARTS), events // PARTS)
        return pltpu.make_async_remote_copy(
            src_ref=held.at[source, rows],
            dst_ref=held.at[slot, rows],
            send_sem=send_sem,
            recv_sem=recv_sem.at[slot, part or 0],
            device_id=(device,),
            device_id_type=pl.DeviceIdType.MESH,
        )

    def arrived(slot, part):
        remote(slot, slot, z_sem.at[part or 0], sibling, part).wait_recv()

    def to_sibling(i):
        return remote(2 * i + 2 - 2 * core, 2 * i + 1, pair_sem.at[i], sibling)

    def sibling_wants(i):
        return 2 * chip + 2 * i + 2 - 2 * core < devices

    def z_copy(part):
        return remote(0, far, z_sem.at[part], me - 2 * per_layer, part)

    def across_copy(d, part):
        return remote(0, 2 * d, layer_sem.at[d - 1, part], me - 2 * d, part)

    def layer_copy(d, source, part):
        return remote(source, 2 * d, layer_sem.at[d - 1, part], in_layer(d), part)

    def relays(d):
        return has_up & (place < d) & (d != 2 * place + 1)

    def ten_copy(part):
        return remote(far, last, ten_sem.at[part], me - 2, part)

    @pl.when(has_down)
    def _():
        for part in range(PARTS):
            z_copy(part).start()

    for d, (down, up) in across.items():
        @pl.when(down)
        def _(d=d):
            for part in range(PARTS):
                across_copy(d, part).start()

    for d in range(per_layer - 1, 0, -1):
        @pl.when(place >= d)
        def _(d=d):
            for part in range(PARTS):
                layer_copy(d, 0, part).start()

    @pl.when(core == 1)
    def _():
        to_sibling(0).start()

    padded = jnp.concatenate(
        [own.astype(jnp.float32), jnp.zeros((events, LANES), jnp.float32)], axis=1
    )
    width = samples + LANES
    for lag in range(LAGS):
        moved = pltpu.roll(padded, (lag - HALF) % width, 1) if lag != HALF else padded
        shifted[lag] = moved[:, :samples].astype(jnp.bfloat16)
    ones = jnp.ones((samples, LANES), jnp.bfloat16)
    high, low = split_squares(own)
    row_scale[...] = lax.rsqrt(
        lax.dot_general(high, ones, NN, preferred_element_type=jnp.float32)
        + lax.dot_general(low, ones, NN, preferred_element_type=jnp.float32)
        + epsilon
    )

    def pass_far():
        for part in range(PARTS):
            @pl.when(has_up)
            def _(part=part):
                arrived(far, part)

            for d in range(per_layer - 1, 0, -1):
                @pl.when(relays(d))
                def _(d=d, part=part):
                    layer_copy(d, far, part).start()

            @pl.when((core == 0) & (chip >= 1) & has_up)
            def _(part=part):
                ten_copy(part).start()

        @pl.when((core == 0) & has_up)
        def _():
            to_sibling(far // 2 - 1).start()

        @pl.when((core == 1) & has_up)
        def _():
            to_sibling(far // 2).start()

    def pass_on(slot):
        @pl.when(2 * chip + slot < devices)
        def _():
            for part in range(PARTS):
                arrived(slot, part)

            @pl.when(core == 0)
            def _():
                to_sibling(slot // 2 - 1).start()

            @pl.when(core == 1)
            def _():
                to_sibling(slot // 2).start()

    def pass_last():
        @pl.when((core == 0) & (me + last < devices))
        def _():
            for part in range(PARTS):
                arrived(last, part)
            to_sibling(last // 2 - 1).start()

    def receive(slot):
        @pl.when(me + slot < devices)
        def _():
            arrived(slot, None)

    def scale_of(slots):
        parts = []
        for slot in slots:
            high, low = split_squares(held[slot])
            rows = jnp.ones((8, samples), jnp.bfloat16)
            total = lax.dot_general(rows, high, NT, preferred_element_type=jnp.float32)
            total += lax.dot_general(rows, low, NT, preferred_element_type=jnp.float32)
            partner_scale = lax.rsqrt(total + epsilon)
            if slot > 0:
                partner_scale *= pair_valid[0, slot - 1].astype(jnp.float32)
            parts.append(row_scale[...] * partner_scale[0:1, :])
        return jnp.concatenate(parts, axis=1)

    first, second = in_order(reach)
    inputs[2].wait()

    def await_slot(slot):
        if slot == 0:
            return
        if slot == far:
            pass_far()
        elif slot % 2 == 0:
            pass_on(slot)
            if slot == far - 2:
                pass_last()
        else:
            receive(slot)

    n = 0
    for slots in first:
        for slot in slots:
            await_slot(slot)
        right = jnp.concatenate([held[slot] for slot in slots], axis=0)
        product = product_of(shifted, right, scale_of(slots))
        for i in range(len(slots)):
            done[n] = product[:, :, i * events : (i + 1) * events]
            n += 1
    n = 0
    for i, slots in enumerate(second):
        for slot in slots:
            await_slot(slot)
            late[n] = held[slot]
            n += 1
        late_scale[i] = scale_of(slots)

    for part in range(PARTS):
        @pl.when(has_down)
        def _(part=part):
            z_copy(part).wait_send()

        for d in range(1, per_layer):
            @pl.when((place >= d) | relays(d))
            def _(d=d, part=part):
                layer_copy(d, 0, part).wait_send()

        for d, (down, up) in across.items():
            @pl.when(down)
            def _(d=d, part=part):
                across_copy(d, part).wait_send()

        @pl.when((core == 0) & (chip >= 1) & has_up)
        def _(part=part):
            ten_copy(part).wait_send()

    for i in range((reach + 1) // 2):
        @pl.when(sibling_wants(i))
        def _(i=i):
            to_sibling(i).wait_send()


def shards(devices, records, filter_taps, live_counts, pair_valid):
    events, samples = records.shape
    reach = pair_valid.shape[1]
    vmem = pl.BlockSpec(memory_space=pltpu.VMEM)
    hbm = pl.BlockSpec(memory_space=pltpu.HBM)
    taps = filter_taps.reshape(1, -1)
    records, taps, pair_valid = [
        pltpu.with_memory_space_constraint(x, pltpu.HBM)
        for x in (records, taps, pair_valid)
    ]
    first, second = in_order(reach)
    done_count = sum(len(slots) for slots in first)
    late_count = sum(len(slots) for slots in second)
    arrays = pl.pallas_call(
        functools.partial(kernel, devices),
        out_shape=[
            pltpu.VMEM((done_count, LAGS, events, events), jnp.bfloat16),
            pltpu.VMEM((LAGS, events, samples), jnp.bfloat16),
            pltpu.VMEM((late_count, events, samples), jnp.bfloat16),
            pltpu.VMEM((len(second), events, 2 * events), jnp.float32),
        ],
        in_specs=[hbm, hbm, pl.BlockSpec(memory_space=pltpu.SMEM), hbm],
        out_specs=[vmem] * 4,
        scratch_shapes=[
            pltpu.VMEM((events, samples), jnp.bfloat16),
            pltpu.VMEM((1, filter_taps.shape[0]), jnp.bfloat16),
            pltpu.SMEM((1, reach), jnp.int32),
            pltpu.VMEM((reach + 2, events, samples), jnp.bfloat16),
            pltpu.VMEM((8, samples), jnp.float32),
            pltpu.VMEM((events, LANES), jnp.float32),
            pltpu.SemaphoreType.DMA((3,)),
            pltpu.SemaphoreType.DMA((PARTS,)),
            pltpu.SemaphoreType.DMA(((reach - 1) // 2 - 1, PARTS)),
            pltpu.SemaphoreType.DMA((PARTS,)),
            pltpu.SemaphoreType.DMA(((reach + 1) // 2,)),
            pltpu.SemaphoreType.DMA((reach + 2, PARTS)),
        ],
        compiler_params=pltpu.CompilerParams(
            collective_id=0, has_side_effects=True, vmem_limit_bytes=24 * 1024 * 1024
        ),
        cost_estimate=pl.CostEstimate(
            flops=2 * (reach + 1) * LAGS * events * events * samples,
            bytes_accessed=2 * (reach + 1) * LAGS * events * events,
            transcendentals=0,
        ),
    )(records, taps, live_counts, pair_valid)
    correlations = pl.pallas_call(
        functools.partial(finish, first, second),
        out_shape=jax.ShapeDtypeStruct((reach + 1, LAGS, events, events), jnp.bfloat16),
        in_specs=[vmem] * 4,
        out_specs=hbm,
        scratch_shapes=[
            pltpu.VMEM((late_count, LAGS, events, events), jnp.bfloat16),
            pltpu.SemaphoreType.DMA((reach + 1,)),
        ],
        compiler_params=pltpu.CompilerParams(vmem_limit_bytes=24 * 1024 * 1024),
    )(*arrays)
    return jnp.transpose(correlations, (2, 0, 1, 3))


def solution(mesh):
    in_specs = (P("ev", None), P(), P("ev"), P("ev", None))
    out_specs = P("ev", None, None, None)
    return jax.shard_map(
        functools.partial(shards, mesh.shape["ev"]),
        mesh=mesh, in_specs=in_specs, out_specs=out_specs, check_vma=False,
    )
```
